256 devices in a mesh: blk: 32 (over z_lo, x, core), users: 8 (over y, z_hi).
Axes of the slice: x: 4, y: 4, z: 8 (z_hi: 2, z_lo: 4; z = z_hi * 4 + z_lo), core: 2. Of those that a mesh axis runs over, the one named last changes fastest.
Arguments:
- interactions: bfloat16 [8192, 8192], P('users', 'blk'), may hold values from -0.125 to 0.125
- tile_mask: int32 [64, 64], P('users', 'blk'), may hold values from 0 to 1
- panel_of: int32 [32], replicated, may hold values from 0 to 31, each once
Outputs:
- gram: float32 [8192, 8192], P('users', 'blk')
The draws below stay inside these ranges and needn't reach their ends.
All inputs are finite; a program needn't handle non-finite values.
Results may differ from the reference program's by a relative error of at most 0.0003.
Values may be sent and summed in bfloat16 or wider, within the bound.
No kernel may reach another device: no remote copies, remote signals or barrier semaphores. Data moves between devices by JAX's collectives and lax.ppermute only.
A program may use at most 128 MiB of HBM per device.

```python
import jax
import jax.numpy as jnp
from jax import lax

TILE = 128
ITEMS = 8192
USERS = 8192
N_BLK = 32


def draw_tile_mask(key, part):
    key = jax.random.fold_in(key, 7)
    level_key, value_key = jax.random.split(key)
    levels = jax.random.randint(level_key, (1, ITEMS // TILE), 0, 4)
    values = jax.random.randint(value_key, (USERS // TILE, ITEMS // TILE), 0, 8)
    return (values < 2 + 2 * levels).astype(jnp.int32)


def raised(array, stream_key, source, target, blocks, factor):
    owner, partner = [(jnp.arange(array.shape[axis_at]) // (array.shape[axis_at] // blocks)).reshape([-1 if axis == axis_at else 1 for axis in range(array.ndim)]) for axis_at in (source, target)]
    chosen = jax.random.permutation(stream_key, blocks)[partner]
    strong = (owner == chosen) | (owner == (partner + blocks // 2) % blocks)
    return jnp.where(strong, factor * array, array)


def level_of(rng, dims, cuts, least, top_value):
    factor_of, own = 1.0, jax.random.fold_in(rng, 6)
    for dim, parts in cuts:
        heights = jnp.exp(jax.random.uniform(jax.random.fold_in(own, dim), (parts,), jnp.float32, least / len(cuts), top_value / len(cuts)))
        factor_of = factor_of * jnp.repeat(heights, dims[dim] // parts).reshape([-1 if axis == dim else 1 for axis in range(len(dims))])
    return factor_of


def noise_with(own_key, extent, deviation, reach, cuts, heavy, kind=jnp.bfloat16):
    array = deviation * jax.random.normal(own_key, extent, jnp.float32)
    if cuts:
        array = array * level_of(own_key, extent, cuts, -0.22, 0.18)
    return jnp.clip(raised(array, jax.random.fold_in(own_key, 3), *heavy), -reach, reach).astype(kind)


def setup_inputs(seed: int = 0) -> dict:
    key_of = jax.random.split(jax.random.key(seed), 4)
    interactions = noise_with(key_of[0], (USERS, ITEMS), USERS ** -0.5, 0.125, ((0, 8), (1, 32)), (0, 1, 32, 2.75))
    tile_mask = draw_tile_mask(jax.random.fold_in(key_of[3], 71), 0)
    panel_of = jax.random.permutation(key_of[2], N_BLK).astype(jnp.int32)
    return {"interactions": interactions, "tile_mask": tile_mask, "panel_of": panel_of}


def reference(interactions, tile_mask, panel_of):
    user_count = interactions.shape[0]
    item_count = interactions.shape[1]
    user_tiles = user_count // TILE
    item_tiles = item_count // TILE
    mask_values = tile_mask.astype(interactions.dtype)
    masked = (interactions.reshape(user_tiles, TILE, item_tiles, TILE) * mask_values[:, None, :, None]).reshape(user_count, item_count)
    panels = panel_of.shape[0]
    width = item_count // panels
    order = jnp.arange(panels, dtype=jnp.int32)
    inverse = jnp.sum(order[None, :] * (panel_of[None, :] == order[:, None]).astype(jnp.int32), axis=1).astype(jnp.int32)
    stacked = masked.reshape(user_count, panels, width)

    def one_panel(source):
        block = lax.dynamic_index_in_dim(stacked, source, 1, keepdims=False)
        return jnp.dot(block.T, masked, preferred_element_type=jnp.float32)

    rows = lax.map(one_panel, inverse)
    return rows.reshape(item_count, item_count)
```

```python
import jax
import jax.numpy as jnp
from jax import lax
from jax.sharding import PartitionSpec as P

TILE = 128
NZ, NX, NC = 4, 4, 2
NY, NH = 4, 2


def blk_pairs(dz=0, dx=0, flip=False):
    pairs = []
    for z in range(NZ):
        for x in range(NX):
            for c in range(NC):
                source = (((z + dz) % NZ) * NX + (x + dx) % NX) * NC + ((1 - c) if flip else c)
                pairs.append((source, (z * NX + x) * NC + c))
    return pairs


def user_pairs(dy=0, flip=False):
    pairs = []
    for y in range(NY):
        for h in range(NH):
            pairs.append((((y + dy) % NY) * NH + ((1 - h) if flip else h), y * NH + h))
    return pairs


def dot_rows(a, b):
    return lax.dot_general(a, b, (((0,), (0,)), ((), ())), preferred_element_type=jnp.float32)


def on_device(interactions, tile_mask, panel_of):
    rows, width = interactions.shape
    panels = panel_of.shape[0]
    mask = jnp.repeat(jnp.repeat(tile_mask.astype(interactions.dtype), TILE, 0), TILE, 1)
    masked = interactions * mask
    b = lax.axis_index("blk")
    u = lax.axis_index("users")
    core = b % NC
    place = b // NC
    y, h = u // NH, u % NH
    n_users = NY * NH
    piece = rows // panels
    places = panels // NC

    halves = masked.reshape(places, NC, piece, width)
    mine = lax.dynamic_index_in_dim(halves, core, 1, keepdims=False)
    other = lax.dynamic_index_in_dim(halves, 1 - core, 1, keepdims=False)
    got = lax.ppermute(other, "blk", blk_pairs(flip=True))
    pair = jnp.where(core == 0, jnp.concatenate([mine, got], -1), jnp.concatenate([got, mine], -1))
    across = lax.ppermute(pair, "users", user_pairs(flip=True))

    spread = lax.all_to_all(masked.reshape(panels, piece, width), "blk", 0, 0, tiled=True)
    inverse = jnp.zeros((panels,), jnp.int32).at[panel_of].set(jnp.arange(panels, dtype=jnp.int32))
    chosen = jnp.take(spread, inverse, axis=0)
    per_user = panels // n_users
    chosen = chosen.reshape(n_users, per_user, piece, width).transpose(0, 2, 1, 3)
    unit = lax.all_to_all(chosen.reshape(n_users, piece, per_user * width), "users", 0, 0, tiled=True)
    unit = unit.reshape(n_users * piece, per_user * width)
    half = unit.shape[0] // 2

    both = jnp.stack([jnp.where(h == 0, pair, across), jnp.where(h == 0, across, pair)], 0)
    up = lax.ppermute(both, "users", user_pairs(dy=1))
    down = lax.ppermute(both, "users", user_pairs(dy=-1))
    far_a = lax.ppermute(up[0], "users", user_pairs(dy=1))
    far_b = lax.ppermute(down[1], "users", user_pairs(dy=-1))
    far = jnp.stack([far_a, far_b], 0)
    cols = jnp.zeros((NY,) + both.shape, both.dtype)
    for dy, part in ((0, both), (1, up), (2, far), (3, down)):
        cols = lax.dynamic_update_slice_in_dim(cols, part[None], (y + dy) % NY, 0)
    cols = cols.reshape(n_users, places, piece, NC * width)

    zl, x = place // NX, place % NX
    total = None

    def add(total, a, dz, dx, lo, hi):
        at = ((zl + dz) % NZ) * NX + (x + dx) % NX
        part = lax.dynamic_index_in_dim(cols, at, 1, keepdims=False)
        part = part.reshape(n_users * piece, NC * width)[lo:hi]
        r = dot_rows(a, part)
        return r if total is None else total + r

    for dz in (0, 1, 3, 2):
        own = unit if dz == 0 else lax.ppermute(unit, "blk", blk_pairs(dz=dz))
        right = lax.ppermute(own, "blk", blk_pairs(dx=1))
        left = lax.ppermute(own, "blk", blk_pairs(dx=-1))
        far_r = lax.ppermute(right[:half], "blk", blk_pairs(dx=1))
        far_l = lax.ppermute(left[half:], "blk", blk_pairs(dx=-1))
        total = add(total, own, dz, 0, 0, 2 * half)
        total = add(total, right, dz, 1, 0, 2 * half)
        total = add(total, left, dz, 3, 0, 2 * half)
        total = add(total, far_r, dz, 2, 0, half)
        total = add(total, far_l, dz, 2, half, 2 * half)
    keep = lax.dynamic_slice_in_dim(total, core * width, width, 1)
    give = lax.dynamic_slice_in_dim(total, (1 - core) * width, width, 1)
    return keep + lax.ppermute(give, "blk", blk_pairs(flip=True))


def solution(mesh):
    return jax.shard_map(
        on_device,
        mesh=mesh,
        in_specs=(P("users", "blk"), P("users", "blk"), P()),
        out_specs=P("users", "blk"),
        check_vma=False,
    )
```

```python
import functools

import jax
import jax.numpy as jnp
from jax import lax
from jax.experimental import pallas as pl
from jax.experimental.pallas import tpu as pltpu
from jax.sharding import Mesh, PartitionSpec as P

TILE = 128
SIZES = {"zl": 4, "x": 4, "c": 2, "y": 4, "zh": 2}
BLK = ("zl", "x", "c")
USERS = ("y", "zh")
LINE = ("zl", "zh")
VMEM = pl.BlockSpec(memory_space=pltpu.VMEM)
SMEM = pl.BlockSpec(memory_space=pltpu.SMEM)
LIMIT = 48 * 1024 * 1024
ROWS = ((0, 512), (512, 512))
GROUPS = ((0, 1, -1, 2, -2), (3, -3, 4))
TAIL = 16
LARGEST = 32768.0


def shift(a, axis, by):
    n = SIZES[axis]
    return lax.ppermute(a, axis, [((i + by) % n, i) for i in range(n)])


def along(a, by):
    n = SIZES["zh"] * SIZES["zl"]
    index = [i % SIZES["zl"] * SIZES["zh"] + i // SIZES["zl"] for i in range(n)]
    return lax.ppermute(a, LINE, [(index[(i + by) % n], index[i]) for i in range(n)])


def tie(a, *others):
    return lax.optimization_barrier((a, *others))[0]


def mask_kernel(core, tiles, full, blocks, ordered):
    rows, width = full.shape
    nz, nx = SIZES["zl"], SIZES["x"]
    piece = blocks.shape[1]
    c = core[0]
    for i in range(rows // TILE):
        for j in range(width // TILE):
            kept = tiles[i, j].astype(jnp.float32).astype(full.dtype)
            cols = pl.ds(j * TILE, TILE)
            value = full[pl.ds(i * TILE, TILE), cols] * kept
            for k in range(TILE // piece):
                t = i * (TILE // piece) + k
                x, z, e = t // (nz * 2), t // 2 % nz, t % 2
                part = value[k * piece:(k + 1) * piece]
                blocks[(z * nx + x) * 2 + e, :, cols] = part
                ordered[x, c ^ e, pl.ds(z * piece, piece), cols] = part


def apply_mask(interactions, tile_mask, core, panels):
    rows, width = interactions.shape
    piece = rows // panels
    nx = SIZES["x"]
    return pl.pallas_call(
        mask_kernel,
        out_shape=(
            jax.ShapeDtypeStruct((panels, piece, width), interactions.dtype),
            jax.ShapeDtypeStruct((nx, 2, rows // nx // 2, width), interactions.dtype),
        ),
        in_specs=[SMEM, SMEM, VMEM],
        out_specs=(VMEM, VMEM),
        name="mask",
    )(core, tile_mask, interactions)


def pick_kernel(order, spread, out):
    per, width = out.shape[3] // spread.shape[2], spread.shape[2]
    for y in range(SIZES["y"]):
        for h in range(SIZES["zh"]):
            for p in range(per):
                at = (y * SIZES["zh"] + h) * per + p
                out[y, h, :, p * width:(p + 1) * width] = spread[order[at]]


def pick(order, spread):
    panels, piece, width = spread.shape
    users = SIZES["y"] * SIZES["zh"]
    return pl.pallas_call(
        pick_kernel,
        out_shape=jax.ShapeDtypeStruct(
            (SIZES["y"], SIZES["zh"], piece, panels // users * width), spread.dtype
        ),
        in_specs=[SMEM, VMEM],
        out_specs=VMEM,
        name="pick",
    )(order, spread)


def product_kernel(groups, n_near, at, *refs):
    nx, ny = SIZES["x"], SIZES["y"]
    sides, refs = refs[:2 * len(groups)], refs[2 * len(groups):]
    near, away, outs = refs[:n_near], refs[n_near:-nx], refs[-nx:]

    def column(refs, dy, here):
        return refs[dy][here] if len(refs) > 1 else refs[0][(at[dy], *here)]

    piece = sides[0].shape[2]
    rows, cols = [], []
    chunk = 0
    for g, size in enumerate(groups):
        for k in range(size):
            low = pl.multiple_of(at[ny + 2 * chunk] * piece, piece)
            same = at[ny + 2 * chunk + 1] == 0
            chunk += 1
            for crel in range(2):
                for dy in range(ny):
                    rows.append(sides[2 * g + crel][k, at[dy]])
                    here = (slice(None), crel, pl.ds(low, piece))
                    cols.append(jnp.where(same, column(near, dy, here), column(away, dy, here)))
    rows = jnp.concatenate(rows, 0).T
    for dx in range(nx):
        b = jnp.concatenate([c[dx] for c in cols], 0)
        r = jnp.dot(rows, b, preferred_element_type=jnp.float32)
        if dx == 0:
            outs[dx][...] = r
            continue
        most = jnp.maximum(jnp.max(jnp.abs(r)), 1e-30)
        power = jnp.floor(jnp.log2(jnp.full((TAIL, r.shape[1]), LARGEST / most, jnp.float32)))
        outs[dx][0, :r.shape[0]] = r * jnp.exp2(power[:1])
        outs[dx][0, r.shape[0]:] = power


def product(at, sides, near, away, lo, size):
    _, ny, piece, _ = sides[0].shape
    nx, width = SIZES["x"], near[0].shape[-1]
    tile = 256
    groups = tuple(a.shape[0] for a in sides[::2])
    n_chunks = sum(groups)
    in_specs = [
        pl.BlockSpec((a.shape[0], ny, piece, tile), lambda i, s: (0, 0, 0, i + lo // tile)) for a in sides
    ]
    for a in (*near, *away):
        in_specs.append(pl.BlockSpec(a.shape, functools.partial(lambda n, i, s: (0,) * n, a.ndim)))
    plain = jax.ShapeDtypeStruct((size, width), jnp.float32)
    packed = jax.ShapeDtypeStruct((size // tile, tile + TAIL, width), jnp.float32)
    depth = 2 * n_chunks * ny * piece
    return pl.pallas_call(
        functools.partial(product_kernel, groups, len(near)),
        out_shape=(plain,) + (packed,) * (nx - 1),
        grid_spec=pltpu.PrefetchScalarGridSpec(
            num_scalar_prefetch=1,
            grid=(size // tile,),
            in_specs=in_specs,
            out_specs=(pl.BlockSpec((tile, width), lambda i, s: (i, 0)),)
            + (pl.BlockSpec((1, tile + TAIL, width), lambda i, s: (i, 0, 0)),) * (nx - 1),
        ),
        compiler_params=pltpu.CompilerParams(vmem_limit_bytes=LIMIT),
        cost_estimate=pl.CostEstimate(
            flops=2 * depth * size * nx * width,
            bytes_accessed=2 * depth * size + 4096 * nx * width + 4 * nx * size * width,
            transcendentals=0,
        ),
        name="product",
    )(at, *sides, *near, *away)


def opened(message):
    tiles, rows, width = message.shape
    body = message[:, :rows - TAIL].astype(jnp.float32)
    power = message[:, rows - TAIL:rows - TAIL + 1].astype(jnp.float32)
    return (body * jnp.exp2(-power)).reshape(tiles * (rows - TAIL), width)


def on_device(interactions, tile_mask, panel_of):
    rows, width = interactions.shape
    panels = panel_of.shape[0]
    x, core, y, zh, zl = (lax.axis_index(name) for name in ("x", "c", "y", "zh", "zl"))
    nx, ny, nz = SIZES["x"], SIZES["y"], SIZES["zl"]
    around = SIZES["zh"] * nz
    ring = zh * nz + zl

    blocks, ordered = apply_mask(interactions, tile_mask, core.reshape(1).astype(jnp.int32), panels)
    spread = lax.all_to_all(blocks, BLK, 0, 0, tiled=True)

    def over_x(a, *after):
        def slice_for(dx):
            return lax.dynamic_index_in_dim(a, (x + dx) % nx, 0, keepdims=False)

        return jnp.stack(
            [slice_for(0)] + [shift(tie(slice_for(-dx), *after), "x", dx) for dx in range(1, nx)], 0
        )

    mine = over_x(ordered)
    near = [mine] + [shift(mine, "y", dy) for dy in range(1, ny)]
    crossed = shift(mine, "zh", 1)
    across = crossed
    away = [lax.all_to_all(jnp.broadcast_to(across[None], (ny, *across.shape)), "y", 0, 0)]

    stored = jnp.arange(panels, dtype=jnp.int32)
    order = jnp.sum(jnp.where(panel_of[None, :] == stored[:, None], stored[None, :], 0), 1).astype(jnp.int32)
    mixed = lax.all_to_all(pick(order, tie(spread, mine)), "y", 0, 0, tiled=True)
    flat = (-1, mixed.shape[-1])

    def side(h):
        return lax.dynamic_index_in_dim(mixed, h, 1, keepdims=False)

    def from_ring(d, *after):
        if d == 0:
            return side(zh)
        dest = (ring - d) % around
        part = side(dest // nz)
        return along(tie(part.reshape(flat), *after), d).reshape(part.shape)

    def where():
        out = [(y + dy) % ny for dy in range(ny)]
        for group in GROUPS:
            for d in group:
                source = (ring + d) % around
                out += [source % nz, (source // nz) ^ zh]
        return jnp.stack(out).astype(jnp.int32)

    held = {0: from_ring(0)}
    for d in (1, -1):
        held[d] = from_ring(d)
    for d in (2, -2):
        held[d] = from_ring(d, across)
    for d in (3, -3):
        held[d] = from_ring(d, across, held[1], held[-1])
    for d in (4,):
        held[d] = from_ring(d, held[1], held[-1], *near)
    sides = []
    for group in GROUPS:
        own = jnp.stack([held[d] for d in group], 0)
        sides += [own, shift(own, "c", 1)]
    done = []
    for lo, size in ROWS:
        total, *sent = product(where(), sides, near, away, lo, size)
        for dx in range(1, nx):
            total = total + opened(shift(sent[dx - 1].astype(jnp.float16), "x", -dx))
        done.append(total)
    return jnp.concatenate(done, 0)


def solution(mesh):
    fine = Mesh(mesh.devices.reshape(tuple(SIZES.values())), tuple(SIZES))
    return jax.shard_map(
        on_device,
        mesh=fine,
        in_specs=(P(USERS, BLK), P(USERS, BLK), P()),
        out_specs=P(USERS, BLK),
        check_vma=False,
    )
```

```python
import functools

import jax
import jax.numpy as jnp
from jax import lax
from jax.experimental import pallas as pl
from jax.experimental.pallas import tpu as pltpu
from jax.sharding import Mesh, PartitionSpec as P

TILE = 128
SIZES = {"zl": 4, "x": 4, "c": 2, "y": 4, "zh": 2}
BLK = ("zl", "x", "c")
USERS = ("y", "zh")
LINE = ("zl", "zh")
VMEM = pl.BlockSpec(memory_space=pltpu.VMEM)
SMEM = pl.BlockSpec(memory_space=pltpu.SMEM)
LIMIT = 48 * 1024 * 1024
ROWS = ((0, 512), (512, 512))
GROUPS = ((0, 1, -1, 2, -2), (3, -3, 4))
TAIL = 16
LARGEST = 32768.0


def shift(a, axis, by):
    n = SIZES[axis]
    return lax.ppermute(a, axis, [((i + by) % n, i) for i in range(n)])


def along(a, by):
    n = SIZES["zh"] * SIZES["zl"]
    index = [i % SIZES["zl"] * SIZES["zh"] + i // SIZES["zl"] for i in range(n)]
    return lax.ppermute(a, LINE, [(index[(i + by) % n], index[i]) for i in range(n)])


def tie(a, *others):
    return lax.optimization_barrier((a, *others))[0]


def mask_kernel(core, tiles, full, blocks, ordered):
    rows, width = full.shape
    nz, nx = SIZES["zl"], SIZES["x"]
    piece = blocks.shape[1]
    c = core[0]
    for i in range(rows // TILE):
        for j in range(width // TILE):
            kept = tiles[i, j].astype(full.dtype)
            cols = pl.ds(j * TILE, TILE)
            value = full[pl.ds(i * TILE, TILE), cols] * kept
            for k in range(TILE // piece):
                t = i * (TILE // piece) + k
                x, z, e = t // (nz * 2), t // 2 % nz, t % 2
                part = value[k * piece:(k + 1) * piece]
                blocks[(z * nx + x) * 2 + e, :, cols] = part
                ordered[x, c ^ e, pl.ds(z * piece, piece), cols] = part


def apply_mask(interactions, tile_mask, core, panels):
    rows, width = interactions.shape
    piece = rows // panels
    nx = SIZES["x"]
    return pl.pallas_call(
        mask_kernel,
        out_shape=(
            jax.ShapeDtypeStruct((panels, piece, width), interactions.dtype),
            jax.ShapeDtypeStruct((nx, 2, rows // nx // 2, width), interactions.dtype),
        ),
        in_specs=[SMEM, SMEM, VMEM],
        out_specs=(VMEM, VMEM),
        name="mask",
    )(core, tile_mask.astype(jnp.float32), interactions)


def pick_kernel(order, spread, out):
    per, width = out.shape[3] // spread.shape[2], spread.shape[2]
    for y in range(SIZES["y"]):
        for h in range(SIZES["zh"]):
            for p in range(per):
                at = (y * SIZES["zh"] + h) * per + p
                out[y, h, :, p * width:(p + 1) * width] = spread[order[at]]


def pick(order, spread):
    panels, piece, width = spread.shape
    users = SIZES["y"] * SIZES["zh"]
    return pl.pallas_call(
        pick_kernel,
        out_shape=jax.ShapeDtypeStruct(
            (SIZES["y"], SIZES["zh"], piece, panels // users * width), spread.dtype
        ),
        in_specs=[SMEM, VMEM],
        out_specs=VMEM,
        name="pick",
    )(order, spread)


def product_kernel(groups, n_near, at, *refs):
    nx, ny = SIZES["x"], SIZES["y"]
    sides, refs = refs[:2 * len(groups)], refs[2 * len(groups):]
    near, away, outs = refs[:n_near], refs[n_near:-nx], refs[-nx:]

    def column(refs, dy, here):
        return refs[dy][here] if len(refs) > 1 else refs[0][(at[dy], *here)]

    piece = sides[0].shape[2]
    rows, cols = [], []
    chunk = 0
    for g, size in enumerate(groups):
        for k in range(size):
            low = pl.multiple_of(at[ny + 2 * chunk] * piece, piece)
            same = at[ny + 2 * chunk + 1] == 0
            chunk += 1
            for crel in range(2):
                for dy in range(ny):
                    rows.append(sides[2 * g + crel][k, at[dy]])
                    here = (slice(None), crel, pl.ds(low, piece))
                    cols.append(jnp.where(same, column(near, dy, here), column(away, dy, here)))
    rows = jnp.concatenate(rows, 0).T
    for dx in range(nx):
        b = jnp.concatenate([c[dx] for c in cols], 0)
        r = jnp.dot(rows, b, preferred_element_type=jnp.float32)
        if dx == 0:
            outs[dx][...] = r
            continue
        most = jnp.maximum(jnp.max(jnp.abs(r)), 1e-30)
        power = jnp.floor(jnp.log2(jnp.full((TAIL, r.shape[1]), LARGEST / most, jnp.float32)))
        outs[dx][0, :r.shape[0]] = r * jnp.exp2(power[:1])
        outs[dx][0, r.shape[0]:] = power


def product(at, sides, near, away, lo, size):
    _, ny, piece, _ = sides[0].shape
    nx, width = SIZES["x"], near[0].shape[-1]
    tile = 256
    groups = tuple(a.shape[0] for a in sides[::2])
    n_chunks = sum(groups)
    in_specs = [
        pl.BlockSpec((a.shape[0], ny, piece, tile), lambda i, s: (0, 0, 0, i + lo // tile)) for a in sides
    ]
    for a in (*near, *away):
        in_specs.append(pl.BlockSpec(a.shape, functools.partial(lambda n, i, s: (0,) * n, a.ndim)))
    plain = jax.ShapeDtypeStruct((size, width), jnp.float32)
    packed = jax.ShapeDtypeStruct((size // tile, tile + TAIL, width), jnp.float32)
    depth = 2 * n_chunks * ny * piece
    return pl.pallas_call(
        functools.partial(product_kernel, groups, len(near)),
        out_shape=(plain,) + (packed,) * (nx - 1),
        grid_spec=pltpu.PrefetchScalarGridSpec(
            num_scalar_prefetch=1,
            grid=(size // tile,),
            in_specs=in_specs,
            out_specs=(pl.BlockSpec((tile, width), lambda i, s: (i, 0)),)
            + (pl.BlockSpec((1, tile + TAIL, width), lambda i, s: (i, 0, 0)),) * (nx - 1),
        ),
        compiler_params=pltpu.CompilerParams(vmem_limit_bytes=LIMIT),
        cost_estimate=pl.CostEstimate(
            flops=2 * depth * size * nx * width,
            bytes_accessed=2 * depth * size + 4096 * nx * width + 4 * nx * size * width,
            transcendentals=0,
        ),
        name="product",
    )(at, *sides, *near, *away)


def opened(message):
    tiles, rows, width = message.shape
    body = message[:, :rows - TAIL].astype(jnp.float32)
    power = message[:, rows - TAIL:rows - TAIL + 1].astype(jnp.float32)
    return (body * jnp.exp2(-power)).reshape(tiles * (rows - TAIL), width)


def on_device(interactions, tile_mask, panel_of):
    rows, width = interactions.shape
    panels = panel_of.shape[0]
    x, core, y, zh, zl = (lax.axis_index(name) for name in ("x", "c", "y", "zh", "zl"))
    nx, ny, nz = SIZES["x"], SIZES["y"], SIZES["zl"]
    around = SIZES["zh"] * nz
    ring = zh * nz + zl

    blocks, ordered = apply_mask(interactions, tile_mask, core.reshape(1).astype(jnp.int32), panels)
    spread = lax.all_to_all(blocks, BLK, 0, 0, tiled=True)

    def over_x(a, *after):
        def slice_for(dx):
            return lax.dynamic_index_in_dim(a, (x + dx) % nx, 0, keepdims=False)

        return jnp.stack(
            [slice_for(0)] + [shift(tie(slice_for(-dx), *after), "x", dx) for dx in range(1, nx)], 0
        )

    mine = over_x(ordered)
    near = [mine] + [shift(mine, "y", dy) for dy in range(1, ny)]
    crossed = shift(mine, "zh", 1)
    across = crossed
    away = [lax.all_to_all(jnp.broadcast_to(across[None], (ny, *across.shape)), "y", 0, 0)]

    stored = jnp.arange(panels, dtype=jnp.int32)
    order = jnp.sum(jnp.where(panel_of[None, :] == stored[:, None], stored[None, :], 0), 1).astype(jnp.int32)
    mixed = lax.all_to_all(pick(order, spread), "y", 0, 0, tiled=True)
    flat = (-1, mixed.shape[-1])

    def side(h):
        return lax.dynamic_index_in_dim(mixed, h, 1, keepdims=False)

    def from_ring(d, *after):
        if d == 0:
            return side(zh)
        dest = (ring - d) % around
        part = side(dest // nz)
        return along(tie(part.reshape(flat), *after), d).reshape(part.shape)

    def where():
        out = [(y + dy) % ny for dy in range(ny)]
        for group in GROUPS:
            for d in group:
                source = (ring + d) % around
                out += [source % nz, (source // nz) ^ zh]
        return jnp.stack(out).astype(jnp.int32)

    held = {0: from_ring(0)}
    for d in (-1, 1):
        held[d] = from_ring(d)
    for d in (2, -2):
        held[d] = from_ring(d, across)
    for d in (-3, 3):
        held[d] = from_ring(d, across, held[1], held[-1])
    for d in (4,):
        held[d] = from_ring(d, held[1], held[-1], *near)
    sides = []
    for group in GROUPS:
        own = jnp.stack([held[d] for d in group], 0)
        sides += [own, shift(own, "c", 1)]
    done = []
    for lo, size in ROWS:
        total, *sent = product(where(), sides, near, away, lo, size)
        for dx in range(1, nx):
            total = total + opened(shift(sent[dx - 1].astype(jnp.float16), "x", -dx))
        done.append(total)
    return jnp.concatenate(done, 0)


def solution(mesh):
    fine = Mesh(mesh.devices.reshape(tuple(SIZES.values())), tuple(SIZES))
    return jax.shard_map(
        on_device,
        mesh=fine,
        in_specs=(P(USERS, BLK), P(USERS, BLK), P()),
        out_specs=P(USERS, BLK),
        check_vma=False,
    )
```

```python
import functools

import jax
import jax.numpy as jnp
from jax import lax
from jax.experimental import pallas as pl
from jax.experimental.pallas import tpu as pltpu
from jax.sharding import Mesh, PartitionSpec as P

TILE = 128
SIZES = {"zl": 4, "x": 4, "c": 2, "y": 4, "zh": 2}
BLK = ("zl", "x", "c")
USERS = ("y", "zh")
LINE = ("zl", "zh")
VMEM = pl.BlockSpec(memory_space=pltpu.VMEM)
SMEM = pl.BlockSpec(memory_space=pltpu.SMEM)
LIMIT = 48 * 1024 * 1024
ROWS = ((0, 512), (512, 512))
GROUPS = ((0, 1, -1, 2, -2), (3, -3, 4))
TAIL = 16
LARGEST = 32768.0


def shift(a, axis, by):
    n = SIZES[axis]
    return lax.ppermute(a, axis, [((i + by) % n, i) for i in range(n)])


def along(a, by):
    n = SIZES["zh"] * SIZES["zl"]
    index = [i % SIZES["zl"] * SIZES["zh"] + i // SIZES["zl"] for i in range(n)]
    return lax.ppermute(a, LINE, [(index[(i + by) % n], index[i]) for i in range(n)])


def tie(a, *others):
    return lax.optimization_barrier((a, *others))[0]


def mask_kernel(core, tiles, full, blocks, ordered):
    rows, width = full.shape
    nz, nx = SIZES["zl"], SIZES["x"]
    piece = blocks.shape[1]
    c = core[0]
    for i in range(rows // TILE):
        for j in range(width // TILE):
            kept = tiles[i, j].astype(full.dtype)
            cols = pl.ds(j * TILE, TILE)
            value = full[pl.ds(i * TILE, TILE), cols] * kept
            for k in range(TILE // piece):
                t = i * (TILE // piece) + k
                x, z, e = t // (nz * 2), t // 2 % nz, t % 2
                part = value[k * piece:(k + 1) * piece]
                blocks[(z * nx + x) * 2 + e, :, cols] = part
                ordered[x, c ^ e, pl.ds(z * piece, piece), cols] = part


def apply_mask(interactions, tile_mask, core, panels):
    rows, width = interactions.shape
    piece = rows // panels
    nx = SIZES["x"]
    return pl.pallas_call(
        mask_kernel,
        out_shape=(
            jax.ShapeDtypeStruct((panels, piece, width), interactions.dtype),
            jax.ShapeDtypeStruct((nx, 2, rows // nx // 2, width), interactions.dtype),
        ),
        in_specs=[SMEM, SMEM, VMEM],
        out_specs=(VMEM, VMEM),
        name="mask",
    )(core, tile_mask.astype(jnp.float32), interactions)


def pick_kernel(order, spread, out):
    per, width = out.shape[3] // spread.shape[2], spread.shape[2]
    for y in range(SIZES["y"]):
        for h in range(SIZES["zh"]):
            for p in range(per):
                at = (y * SIZES["zh"] + h) * per + p
                out[y, h, :, p * width:(p + 1) * width] = spread[order[at]]


def pick(order, spread):
    panels, piece, width = spread.shape
    users = SIZES["y"] * SIZES["zh"]
    return pl.pallas_call(
        pick_kernel,
        out_shape=jax.ShapeDtypeStruct(
            (SIZES["y"], SIZES["zh"], piece, panels // users * width), spread.dtype
        ),
        in_specs=[SMEM, VMEM],
        out_specs=VMEM,
        name="pick",
    )(order, spread)


def product_kernel(groups, n_near, at, *refs):
    nx, ny = SIZES["x"], SIZES["y"]
    sides, refs = refs[:2 * len(groups)], refs[2 * len(groups):]
    near, away, outs = refs[:n_near], refs[n_near:-nx], refs[-nx:]

    def column(refs, dy, here):
        return refs[dy][here] if len(refs) > 1 else refs[0][(at[dy], *here)]

    piece = sides[0].shape[2]
    rows, cols = [], []
    chunk = 0
    for g, size in enumerate(groups):
        for k in range(size):
            low = pl.multiple_of(at[ny + 2 * chunk] * piece, piece)
            same = at[ny + 2 * chunk + 1] == 0
            chunk += 1
            for crel in range(2):
                for dy in range(ny):
                    rows.append(sides[2 * g + crel][k, at[dy]])
                    here = (slice(None), crel, pl.ds(low, piece))
                    cols.append(jnp.where(same, column(near, dy, here), column(away, dy, here)))
    rows = jnp.concatenate(rows, 0).T
    for dx in range(nx):
        b = jnp.concatenate([c[dx] for c in cols], 0)
        r = jnp.dot(rows, b, preferred_element_type=jnp.float32)
        if dx == 0:
            outs[dx][...] = r
            continue
        most = jnp.maximum(jnp.max(jnp.abs(r)), 1e-30)
        power = jnp.floor(jnp.log2(jnp.full((TAIL, r.shape[1]), LARGEST / most, jnp.float32)))
        outs[dx][0, :r.shape[0]] = r * jnp.exp2(power[:1])
        outs[dx][0, r.shape[0]:] = power


def product(at, sides, near, away, lo, size):
    _, ny, piece, _ = sides[0].shape
    nx, width = SIZES["x"], near[0].shape[-1]
    tile = 256
    groups = tuple(a.shape[0] for a in sides[::2])
    n_chunks = sum(groups)
    in_specs = [
        pl.BlockSpec((a.shape[0], ny, piece, tile), lambda i, s: (0, 0, 0, i + lo // tile)) for a in sides
    ]
    for a in (*near, *away):
        in_specs.append(pl.BlockSpec(a.shape, functools.partial(lambda n, i, s: (0,) * n, a.ndim)))
    plain = jax.ShapeDtypeStruct((size, width), jnp.float32)
    packed = jax.ShapeDtypeStruct((size // tile, tile + TAIL, width), jnp.float32)
    depth = 2 * n_chunks * ny * piece
    return pl.pallas_call(
        functools.partial(product_kernel, groups, len(near)),
        out_shape=(plain,) + (packed,) * (nx - 1),
        grid_spec=pltpu.PrefetchScalarGridSpec(
            num_scalar_prefetch=1,
            grid=(size // tile,),
            in_specs=in_specs,
            out_specs=(pl.BlockSpec((tile, width), lambda i, s: (i, 0)),)
            + (pl.BlockSpec((1, tile + TAIL, width), lambda i, s: (i, 0, 0)),) * (nx - 1),
        ),
        compiler_params=pltpu.CompilerParams(vmem_limit_bytes=LIMIT),
        cost_estimate=pl.CostEstimate(
            flops=2 * depth * size * nx * width,
            bytes_accessed=2 * depth * size + 4096 * nx * width + 4 * nx * size * width,
            transcendentals=0,
        ),
        name="product",
    )(at, *sides, *near, *away)


def opened(message):
    tiles, rows, width = message.shape
    body = message[:, :rows - TAIL].astype(jnp.float32)
    power = message[:, rows - TAIL:rows - TAIL + 1].astype(jnp.float32)
    return (body * jnp.exp2(-power)).reshape(tiles * (rows - TAIL), width)


def on_device(interactions, tile_mask, panel_of):
    rows, width = interactions.shape
    panels = panel_of.shape[0]
    x, core, y, zh, zl = (lax.axis_index(name) for name in ("x", "c", "y", "zh", "zl"))
    nx, ny, nz = SIZES["x"], SIZES["y"], SIZES["zl"]
    around = SIZES["zh"] * nz
    ring = zh * nz + zl

    blocks, ordered = apply_mask(interactions, tile_mask, core.reshape(1).astype(jnp.int32), panels)
    spread = lax.all_to_all(blocks, BLK, 0, 0, tiled=True)

    def over_x(a, *after):
        def slice_for(dx):
            return lax.dynamic_index_in_dim(a, (x + dx) % nx, 0, keepdims=False)

        return jnp.stack(
            [slice_for(0)] + [shift(tie(slice_for(-dx), *after), "x", dx) for dx in range(1, nx)], 0
        )

    mine = over_x(ordered)
    near = [mine] + [shift(mine, "y", dy) for dy in range(1, ny)]
    crossed = shift(mine, "zh", 1)
    across = crossed
    away = [lax.all_to_all(jnp.broadcast_to(across[None], (ny, *across.shape)), "y", 0, 0)]

    stored = jnp.arange(panels, dtype=jnp.int32)
    order = jnp.sum(jnp.where(panel_of[None, :] == stored[:, None], stored[None, :], 0), 1).astype(jnp.int32)
    mixed = lax.all_to_all(pick(order, spread), "y", 0, 0, tiled=True)
    flat = (-1, mixed.shape[-1])

    def side(h):
        return lax.dynamic_index_in_dim(mixed, h, 1, keepdims=False)

    def from_ring(d, *after):
        if d == 0:
            return side(zh)
        dest = (ring - d) % around
        part = side(dest // nz)
        return along(tie(part.reshape(flat), *after), d).reshape(part.shape)

    def where():
        out = [(y + dy) % ny for dy in range(ny)]
        for group in GROUPS:
            for d in group:
                source = (ring + d) % around
                out += [source % nz, (source // nz) ^ zh]
        return jnp.stack(out).astype(jnp.int32)

    held = {0: from_ring(0)}
    for d in (-1, 1):
        held[d] = from_ring(d)
    for d in (2, -2):
        held[d] = from_ring(d, across)
    for d in (-3, 3):
        held[d] = from_ring(d, across, held[1], held[-1])
    for d in (4,):
        held[d] = from_ring(d, held[1], held[-1], *near)
    sides = []
    for group in GROUPS:
        own = jnp.stack([held[d] for d in group], 0)
        sides += [own, shift(own, "c", 1)]
    done = []
    for lo, size in ROWS:
        total, *sent = product(where(), sides, near, away, lo, size)
        for dx in (2, 1, 3):
            total = total + opened(shift(sent[dx - 1].astype(jnp.float16), "x", -dx))
        done.append(total)
    return jnp.concatenate(done, 0)


def solution(mesh):
    fine = Mesh(mesh.devices.reshape(tuple(SIZES.values())), tuple(SIZES))
    return jax.shard_map(
        on_device,
        mesh=fine,
        in_specs=(P(USERS, BLK), P(USERS, BLK), P()),
        out_specs=P(USERS, BLK),
        check_vma=False,
    )
```
